32 devices in a mesh: ctx: 16 (over z, x, core), grp: 2 (over y).
Axes of the slice: x: 2, y: 2, z: 4, core: 2. Of those that a mesh axis runs over, the one named last changes fastest.
Arguments:
- query_in: bfloat16 [4096, 4096], P('grp', 'ctx'), may hold values from -6 to 6
- key_in: bfloat16 [4096, 4096], P('grp', 'ctx'), may hold values from -6 to 6
- value_in: bfloat16 [4096, 4096], P('grp', 'ctx'), may hold values from -6 to 6
- cotangent: bfloat16 [4096, 4096], P('grp', 'ctx'), may hold values from -6 to 6
- conv_filter: float32 [256, 4096], P(None, 'ctx'), may hold values from -0.9 to 0.9
Outputs:
- gated_out: bfloat16 [4096, 4096], P('grp', 'ctx')
- grad_query: bfloat16 [4096, 4096], P('grp', 'ctx')
- grad_key: bfloat16 [4096, 4096], P('grp', 'ctx')
- grad_value: bfloat16 [4096, 4096], P('grp', 'ctx')
- grad_filter: float32 [256, 4096], P(None, 'ctx')
The draws below stay inside these ranges and needn't reach their ends.
All inputs are finite; a program needn't handle non-finite values.
Results may differ from the reference program's by a relative error of at most 0.0058.
Values may be sent and summed in bfloat16 or wider, within the bound.
A program may use at most 128 MiB of HBM per device.

```python
import math
import jax
import jax.numpy as jnp
from jax import lax

C = 4096
GROUP_CH = 16
G = 256
SEQ = 4096


def draw_conv_filter(key, part):
    key = jax.random.fold_in(key, 7)
    key_fast, key_slow, key_weight, key_taps = jax.random.split(key, 4)
    low = math.log(40.0)
    high = math.log(4.0 * SEQ)
    fast_decay = jnp.exp(jax.random.uniform(key_fast, (G, 1), jnp.float32, low, high))
    slow_decay = jnp.exp(jax.random.uniform(key_slow, (G, 1), jnp.float32, math.log(1.0 * SEQ), math.log(4.0 * SEQ)))
    residue = jax.random.uniform(key_weight, (G, 1), jnp.float32, 0.3, 0.6)
    lags = jnp.arange(SEQ, dtype=jnp.float32)[None, :]
    fast_part = jnp.sqrt(2.0 / fast_decay) * jnp.exp(-lags / fast_decay)
    slow_part = residue * jnp.sqrt(2.0 / slow_decay) * jnp.exp(-lags / slow_decay)
    envelope = fast_part + slow_part
    noise = jax.random.truncated_normal(key_taps, -3.0, 3.0, (G, SEQ), jnp.float32)
    return (envelope * noise).astype(jnp.float32)


def shard_levels(rng, extent, shards, least, top_value):
    def one(axis_at, blocks):
        draws = jax.random.uniform(jax.random.fold_in(jax.random.fold_in(rng, 6), axis_at), (blocks,), jnp.float32, least / len(shards), top_value / len(shards))
        return jnp.repeat(jnp.exp(draws), extent[axis_at] // blocks).reshape((-1,) + (1,) * (len(extent) - axis_at - 1))

    level = one(*shards[0])
    for cut in shards[1:]:
        level = level * one(*cut)
    return level


def gaussian(rng, shape, deviation, limit, pieces=(), kind=jnp.bfloat16):
    result = deviation * jax.random.normal(rng, shape, jnp.float32)
    if pieces:
        result = result * shard_levels(rng, shape, pieces, -0.22, 0.18)
    return jnp.clip(result, -limit, limit).astype(kind)


def setup_inputs(seed: int = 0) -> dict:
    splits = jax.random.split(jax.random.key(seed), 6)
    return {
        "query_in": gaussian(splits[0], (C, SEQ), 1.0, 6.0, ((0, 2), (1, 16))),
        "key_in": gaussian(splits[1], (C, SEQ), 1.0, 6.0, ((0, 2), (1, 16))),
        "value_in": gaussian(splits[2], (C, SEQ), 1.0, 6.0, ((0, 2), (1, 16))),
        "cotangent": gaussian(splits[3], (C, SEQ), 1.0, 6.0, ((0, 2), (1, 16))),
        "conv_filter": draw_conv_filter(jax.random.fold_in(splits[5], 71), 0),
    }


def reference(query_in, key_in, value_in, cotangent, conv_filter):
    flt = jnp.float32
    total = 2 * SEQ
    mixed = (key_in.astype(flt) * value_in.astype(flt)).astype(jnp.bfloat16)
    taps = jnp.repeat(conv_filter, GROUP_CH, axis=0)
    spec_mixed = jnp.fft.rfft(mixed.astype(flt), n=total, axis=1)
    spec_taps = jnp.fft.rfft(taps, n=total, axis=1)
    conv = jnp.fft.irfft(spec_mixed * spec_taps, n=total, axis=1)[:, :SEQ].astype(jnp.bfloat16)
    gated_out = (query_in.astype(flt) * conv.astype(flt)).astype(jnp.bfloat16)
    grad_query = (cotangent.astype(flt) * conv.astype(flt)).astype(jnp.bfloat16)
    dconv = (cotangent.astype(flt) * query_in.astype(flt)).astype(jnp.bfloat16)
    spec_dconv = jnp.fft.rfft(dconv.astype(flt), n=total, axis=1)
    dmixed = jnp.fft.irfft(spec_dconv * jnp.conj(spec_taps), n=total, axis=1)[:, :SEQ].astype(jnp.bfloat16)
    grad_key = (dmixed.astype(flt) * value_in.astype(flt)).astype(jnp.bfloat16)
    grad_value = (dmixed.astype(flt) * key_in.astype(flt)).astype(jnp.bfloat16)
    dtaps = jnp.fft.irfft(spec_dconv * jnp.conj(spec_mixed), n=total, axis=1)[:, :SEQ]
    grad_filter = lax.optimization_barrier(jnp.sum(dtaps.reshape(G, GROUP_CH, SEQ), axis=1)) / math.sqrt(GROUP_CH * SEQ)
    return (gated_out, grad_query, grad_key, grad_value, grad_filter.astype(flt))
```

```python
import functools
import math

import jax
import jax.numpy as jnp
from jax import lax
from jax.experimental import pallas as pl
from jax.experimental.pallas import tpu as pltpu
from jax.sharding import PartitionSpec as P

GROUP_CH = 16
HALF = 128
BF = jnp.bfloat16
F32 = jnp.float32


def build_toeplitz(taps_row, toep):
    seq = taps_row.shape[1]
    wide = jnp.broadcast_to(taps_row, (HALF, seq))
    rolled = pltpu.roll(wide, 0, 1, stride=1, stride_axis=0)
    row = lax.broadcasted_iota(jnp.int32, (HALF, HALF), 0)
    lane = lax.broadcasted_iota(jnp.int32, (HALF, HALF), 1)
    toep[:, :HALF] = jnp.zeros((HALF, HALF), BF)
    toep[:, HALF : 2 * HALF] = jnp.where(lane >= row, rolled[:, :HALF], 0.0).astype(BF)
    toep[:, 2 * HALF :] = rolled[:, HALF:].astype(BF)


def toeplitz_block(toep, lag, size):
    at = lag * size
    return jnp.concatenate(
        [toep[:, HALF + at : HALF + at + size], toep[:, at : at + size]], axis=0
    )


def group_step(n, size, x_ref, d_ref, f_ref, conv_ref, dmix_ref, part_ref, toep, dpad, acc, acc2):
    rows = n * GROUP_CH
    seq = n * size
    x = x_ref[...].reshape(rows, size)
    d = d_ref[...].reshape(rows, size)
    build_toeplitz(f_ref[0], toep)
    dpad[:rows] = d
    dpad[rows:] = jnp.zeros((rows, size), BF)
    xt = x.T
    pieces = []
    held = None
    for lag in range(n):
        prod = jnp.dot(
            xt, dpad[lag * GROUP_CH : lag * GROUP_CH + rows], preferred_element_type=F32
        )
        top, bottom = prod[:HALF], prod[HALF:]
        if held is not None:
            pieces.append(held + bottom[:, :HALF])
        pieces.append(top[:, :HALF] + bottom[:, HALF:])
        held = top[:, HALF:]
    pieces.append(held)
    pieces.append(jnp.zeros((HALF, HALF), F32))
    total = None
    for r in range(HALF // 8):
        line = jnp.concatenate([p[8 * r : 8 * r + 8] for p in pieces], axis=1)
        if r:
            line = pltpu.roll(line, seq + HALF - 8 * r, 1)
        total = line if total is None else total + line
    out = total[0:1, :]
    for s in range(1, 8):
        out = out + pltpu.roll(total, seq + HALF - s, 1)[s : s + 1, :]
    part_ref[0] = out[:, :seq]
    for lag in range(n):
        keep = rows - lag * GROUP_CH
        block = toeplitz_block(toep, lag, size)
        fwd = jnp.dot(x[:keep], block, preferred_element_type=F32)
        bwd = lax.dot_general(
            d[rows - keep :], block, (((1,), (1,)), ((), ())), preferred_element_type=F32
        )
        if lag == 0:
            acc[...] = fwd
            acc2[...] = bwd
        else:
            acc[rows - keep :] += fwd
            acc2[:keep] += bwd
    conv_ref[...] = acc[...].astype(BF).reshape(n, GROUP_CH, size)
    dmix_ref[...] = acc2[...].astype(BF).reshape(n, GROUP_CH, size)


def convolve(x, d, taps):
    n, width, size = x.shape
    groups = width // GROUP_CH
    rows = n * GROUP_CH
    seq = n * size
    wide_spec = pl.BlockSpec((n, GROUP_CH, size), lambda g: (0, g, 0))
    row_spec = pl.BlockSpec((1, 1, seq), lambda g: (g, 0, 0))
    return pl.pallas_call(
        functools.partial(group_step, n, size),
        grid=(groups,),
        out_shape=(
            jax.ShapeDtypeStruct(x.shape, BF),
            jax.ShapeDtypeStruct(x.shape, BF),
            jax.ShapeDtypeStruct((groups, 1, seq), F32),
        ),
        in_specs=[wide_spec, wide_spec, row_spec],
        out_specs=(wide_spec, wide_spec, row_spec),
        scratch_shapes=[
            pltpu.VMEM((HALF, HALF + seq), BF),
            pltpu.VMEM((2 * rows, size), BF),
            pltpu.VMEM((rows, size), F32),
            pltpu.VMEM((rows, size), F32),
        ],
        compiler_params=pltpu.CompilerParams(vmem_limit_bytes=40 * 1024 * 1024),
        cost_estimate=pl.CostEstimate(
            flops=6 * groups * rows * size * seq, bytes_accessed=8 * n * width * size, transcendentals=0
        ),
    )(x, d, taps)


def swap(blocks):
    return lax.all_to_all(blocks, "ctx", split_axis=0, concat_axis=0, tiled=True)


def per_device(query_in, key_in, value_in, cotangent, conv_filter):
    rows_grp, size = query_in.shape
    n = lax.axis_size("ctx")
    seq = size * n
    width = rows_grp // n
    groups = width // GROUP_CH
    group_dev = rows_grp // GROUP_CH
    blocks = (n, width, size)
    mine = lax.dynamic_slice_in_dim(conv_filter, lax.axis_index("grp") * group_dev, group_dev, 0)
    taps = swap(mine.reshape(n, groups, size))
    taps = jnp.transpose(taps, (1, 0, 2)).reshape(groups, 1, seq)
    q, k = query_in.astype(F32), key_in.astype(F32)
    v, c = value_in.astype(F32), cotangent.astype(F32)
    mixed = swap((k * v).astype(BF).reshape(blocks))
    dconv = swap((c * q).astype(BF).reshape(blocks))
    conv, dmixed, part = convolve(mixed, dconv, taps)
    conv = swap(conv).reshape(rows_grp, size).astype(F32)
    dmixed = swap(dmixed).reshape(rows_grp, size).astype(F32)
    part = swap(jnp.transpose(part.reshape(groups, n, size), (1, 0, 2))).reshape(group_dev, size)
    grad_filter = lax.all_gather(part, "grp", axis=0, tiled=True) / math.sqrt(GROUP_CH * seq)
    return (
        (q * conv).astype(BF),
        (c * conv).astype(BF),
        (dmixed * v).astype(BF),
        (dmixed * k).astype(BF),
        grad_filter,
    )


def solution(mesh):
    wide = P("grp", "ctx")
    return jax.shard_map(
        per_device,
        mesh=mesh,
        in_specs=(wide, wide, wide, wide, P(None, "ctx")),
        out_specs=(wide, wide, wide, wide, P(None, "ctx")),
        check_vma=False,
    )
```

```python
import functools
import math

import jax
import jax.numpy as jnp
from jax import lax
from jax.experimental import pallas as pl
from jax.experimental.pallas import tpu as pltpu
from jax.sharding import PartitionSpec as P

GROUP_CH = 16
HALF = 128
BF = jnp.bfloat16
F32 = jnp.float32
MESH = pl.DeviceIdType.MESH
CHUNKS = 4


def build_toeplitz(taps_row, toep):
    seq = taps_row.shape[1]
    wide = jnp.broadcast_to(taps_row, (HALF, seq))
    rolled = pltpu.roll(wide, 0, 1, stride=1, stride_axis=0)
    row = lax.broadcasted_iota(jnp.int32, (HALF, HALF), 0)
    lane = lax.broadcasted_iota(jnp.int32, (HALF, HALF), 1)
    toep[:, :HALF] = jnp.zeros((HALF, HALF), BF)
    toep[:, HALF : 2 * HALF] = jnp.where(lane >= row, rolled[:, :HALF], 0.0).astype(BF)
    toep[:, 2 * HALF :] = rolled[:, HALF:].astype(BF)


def toeplitz_block(toep, lag, size):
    at = lag * size
    return jnp.concatenate(
        [toep[:, HALF + at : HALF + at + size], toep[:, at : at + size]], axis=0
    )


def diagonal_sums(pieces, seq):
    total = None
    for r in range(HALF // 8):
        line = jnp.concatenate([p[8 * r : 8 * r + 8] for p in pieces], axis=1)
        if r:
            line = pltpu.roll(line, seq + HALF - 8 * r, 1)
        total = line if total is None else total + line
    out = total[0:1, :]
    for s in range(1, 8):
        out = out + pltpu.roll(total, seq + HALF - s, 1)[s : s + 1, :]
    return out[:, :seq]


def nn_dot(a, b):
    return jnp.dot(a, b, preferred_element_type=F32)


def nt_dot(a, b):
    return lax.dot_general(a, b, (((1,), (1,)), ((), ())), preferred_element_type=F32)


def kernel(
    n, grps, width, chunks, size,
    q_ref, k_ref, v_ref, c_ref, f_ref,
    gated_ref, gq_ref, gk_ref, gv_ref, gf_ref,
    mixed_st, dconv_st, xb, db, tapb, conv_st, dmix_st, conv_rc, dmix_rc,
    part_st, part_rc, filt_st, filt_rc, toep, dpad, acc, acc2,
    tap_s, tap_r, x_s, x_r, d_s, d_r, cv_s, cv_r, dm_s, dm_r, pt_s, pt_r, fl_s, fl_r,
):
    me = lax.axis_index("ctx")
    grp = lax.axis_index("grp")
    h = n // 2
    side, lane = me // h, lax.rem(me, h)
    cw = width // chunks
    gpc = cw // GROUP_CH
    rows = h * GROUP_CH
    seq = n * size

    barrier = pltpu.get_barrier_semaphore()

    @pl.loop(1, n)
    def _(r):
        pl.semaphore_signal(barrier, inc=1, device_id={"ctx": lax.rem(me + r, n)}, device_id_type=MESH)

    @pl.loop(1, grps)
    def _(r):
        pl.semaphore_signal(barrier, inc=1, device_id={"grp": lax.rem(grp + r, grps)}, device_id_type=MESH)

    def send(src, dst, ssem, rsem, to):
        pltpu.make_async_remote_copy(
            src_ref=src, dst_ref=dst, send_sem=ssem, recv_sem=rsem,
            device_id={"ctx": to}, device_id_type=MESH,
        ).start()

    def drain(ref, sem):
        pltpu.make_async_copy(ref, ref, sem).wait()

    def product(c):
        @pl.loop(0, h)
        def _(i):
            at = pl.ds(pl.multiple_of(i * width + c * cw, GROUP_CH), cw)
            mixed_st[at, :] = (k_ref[at, :].astype(F32) * v_ref[at, :].astype(F32)).astype(BF)
            dconv_st[at, :] = (c_ref[at, :].astype(F32) * q_ref[at, :].astype(F32)).astype(BF)

    def ship(c):
        def block(st, to):
            return st.at[pl.ds(pl.multiple_of(lax.rem(to, h) * width + c * cw, GROUP_CH), cw)]

        def to_other(st, buf, ssem, rsem):
            @pl.loop(0, h)
            def _(r):
                to = (1 - side) * h + lax.rem(lane + r, h)
                send(block(st, to), buf.at[c, me], ssem.at[c], rsem.at[c], to)

        @pl.when(side == 0)
        def _():
            to_other(mixed_st, xb, x_s, x_r)

        @pl.when(side == 1)
        def _():
            to_other(dconv_st, db, d_s, d_r)

        @pl.loop(1, h)
        def _(r):
            to = side * h + lax.rem(lane + r, h)
            send(block(mixed_st, to), xb.at[c, me], x_s.at[c], x_r.at[c], to)
            send(block(dconv_st, to), db.at[c, me], d_s.at[c], d_r.at[c], to)

        own = pl.ds(pl.multiple_of(lane * width + c * cw, GROUP_CH), cw)
        xb[c, me] = mixed_st[own, :]
        db[c, me] = dconv_st[own, :]

    product(0)
    pl.semaphore_wait(barrier, n - 1 + grps - 1)

    @pl.loop(1, n)
    def _(r):
        to = lax.rem(me + r, n)
        send(f_ref.at[lax.rem(to, h)], tapb.at[me], tap_s, tap_r, to)

    tapb[me] = f_ref[lane]
    ship(0)

    @pl.loop(1, chunks)
    def _(c):
        product(c)
        ship(c)

    drain(tapb.at[pl.ds(0, n - 1)], tap_r)

    def finish(c, few, few_sem, many, many_sem):
        drain(few.at[c, pl.ds(0, h - 1)], few_sem.at[c])
        drain(many.at[c, pl.ds(0, n - 1)], many_sem.at[c])

    def arrived(c):
        @pl.when(side == 0)
        def _():
            finish(c, xb, x_r, db, d_r)

        @pl.when(side == 1)
        def _():
            finish(c, db, d_r, xb, x_r)

    def departed(c):
        @pl.when(side == 0)
        def _():
            finish(c, db, d_s, xb, x_s)

        @pl.when(side == 1)
        def _():
            finish(c, xb, x_s, db, d_s)

    dpad[rows:] = jnp.zeros((2 * rows, size), BF)

    def group(c, g):
        at = pl.ds(pl.multiple_of(g * GROUP_CH, GROUP_CH), GROUP_CH)
        mine = pl.ds(side * h, h)
        x = xb[c, mine, at, :].reshape(rows, size)
        d = db[c, mine, at, :].reshape(rows, size)
        which = pl.ds(c * gpc + g, 1)
        build_toeplitz(jnp.concatenate([tapb[j, which, :] for j in range(n)], axis=1), toep)
        dpad[:rows] = d

        @pl.when(side == 0)
        def _():
            dpad[rows : 2 * rows] = db[c, h:, at, :].reshape(rows, size)

        xt = x.T
        pieces = []
        held = None
        for lag in range(n):
            prod = nn_dot(xt, dpad[lag * GROUP_CH : lag * GROUP_CH + rows])
            top, bottom = prod[:HALF], prod[HALF:]
            if held is not None:
                pieces.append(held + bottom[:, :HALF])
            pieces.append(top[:, :HALF] + bottom[:, HALF:])
            held = top[:, HALF:]
        pieces.append(held)
        pieces.append(jnp.zeros((HALF, HALF), F32))
        sums = diagonal_sums(pieces, seq)
        for j in range(n):
            part_st[c, j, pl.ds(g, 1), :] = sums[:, j * size : (j + 1) * size]
        for lag in range(h):
            keep = rows - lag * GROUP_CH
            block = toeplitz_block(toep, lag, size)
            fwd = nn_dot(x[:keep], block)
            bwd = nt_dot(d[rows - keep :], block)
            if lag == 0:
                acc[...] = fwd
                acc2[...] = bwd
            else:
                acc[rows - keep :] += fwd
                acc2[:keep] += bwd

        @pl.when(side == 1)
        def _():
            low = xb[c, :h, at, :].reshape(rows, size)
            for lag in range(1, n):
                block = toeplitz_block(toep, lag, size)
                cut = GROUP_CH * (lag if lag <= h else lag - h)
                if lag <= h:
                    acc[:cut] += nn_dot(low[rows - cut :], block)
                else:
                    acc[cut:] += nn_dot(low[: rows - cut], block)

        @pl.when(side == 0)
        def _():
            high = db[c, h:, at, :].reshape(rows, size)
            for lag in range(1, n):
                block = toeplitz_block(toep, lag, size)
                cut = GROUP_CH * (lag if lag <= h else lag - h)
                if lag <= h:
                    acc2[rows - cut :] += nt_dot(high[:cut], block)
                else:
                    acc2[: rows - cut] += nt_dot(high[cut:], block)

        conv_st[c, :, at, :] = acc[...].astype(BF).reshape(h, GROUP_CH, size)
        dmix_st[c, :, at, :] = acc2[...].astype(BF).reshape(h, GROUP_CH, size)

    @pl.loop(0, chunks)
    def _(c):
        arrived(c)

        @pl.loop(0, gpc)
        def _(g):
            group(c, g)

        own = pl.ds(pl.multiple_of(lane * width + c * cw, GROUP_CH), cw)

        @pl.loop(1, h)
        def _(r):
            i = lax.rem(lane + r, h)
            to = side * h + i
            send(conv_st.at[c, i], conv_rc.at[own], cv_s.at[c], cv_r.at[c], to)
            send(dmix_st.at[c, i], dmix_rc.at[own], dm_s.at[c], dm_r.at[c], to)

        @pl.loop(1, n)
        def _(r):
            to = lax.rem(me + r, n)
            send(part_st.at[c, to], part_rc.at[c, me], pt_s.at[c], pt_r.at[c], to)

        conv_rc[own, :] = conv_st[c, lane]
        dmix_rc[own, :] = dmix_st[c, lane]
        part_rc[c, me] = part_st[c, me]

    @pl.loop(0, chunks)
    def _(c):
        drain(conv_st.at[c, pl.ds(0, h - 1)], cv_r.at[c])
        drain(dmix_st.at[c, pl.ds(0, h - 1)], dm_r.at[c])

        @pl.loop(0, h)
        def _(i):
            at = pl.ds(pl.multiple_of(i * width + c * cw, GROUP_CH), cw)
            conv = conv_rc[at, :].astype(F32)
            dmixed = dmix_rc[at, :].astype(F32)
            gated_ref[at, :] = (q_ref[at, :].astype(F32) * conv).astype(BF)
            gq_ref[at, :] = (c_ref[at, :].astype(F32) * conv).astype(BF)
            gk_ref[at, :] = (dmixed * v_ref[at, :].astype(F32)).astype(BF)
            gv_ref[at, :] = (dmixed * k_ref[at, :].astype(F32)).astype(BF)

    scale = 1.0 / math.sqrt(GROUP_CH * seq)

    @pl.loop(0, chunks)
    def _(c):
        drain(part_st.at[c, pl.ds(0, n - 1)], pt_r.at[c])
        filt_st[c] = (part_rc[c, :h] + part_rc[c, h:]) * scale

    @pl.loop(1, grps)
    def _(r):
        pltpu.make_async_remote_copy(
            src_ref=filt_st, dst_ref=filt_rc.at[grp], send_sem=fl_s, recv_sem=fl_r,
            device_id={"grp": lax.rem(grp + r, grps)}, device_id_type=MESH,
        ).start()

    filt_rc[grp] = filt_st[...]

    drain(tapb.at[pl.ds(0, n - 1)], tap_s)

    @pl.loop(0, chunks)
    def _(c):
        departed(c)
        drain(conv_st.at[c, pl.ds(0, h - 1)], cv_s.at[c])
        drain(dmix_st.at[c, pl.ds(0, h - 1)], dm_s.at[c])
        drain(part_st.at[c, pl.ds(0, n - 1)], pt_s.at[c])

    drain(filt_rc.at[pl.ds(0, grps - 1)], fl_r)
    gf_ref[...] = filt_rc[...]
    drain(filt_rc.at[pl.ds(0, grps - 1)], fl_s)


def per_device(query_in, key_in, value_in, cotangent, conv_filter):
    rows_grp, size = query_in.shape
    n, grps = lax.axis_size("ctx"), lax.axis_size("grp")
    h = n // 2
    seq = size * n
    width = rows_grp // h
    groups = width // GROUP_CH
    chunks = min(CHUNKS, groups)
    cw = width // chunks
    gpc = groups // chunks
    group_dev = rows_grp // GROUP_CH
    mine = lax.dynamic_slice_in_dim(conv_filter, lax.axis_index("grp") * group_dev, group_dev, 0)
    rows = h * GROUP_CH
    wide = jax.ShapeDtypeStruct((rows_grp, size), BF)
    vmem = pl.BlockSpec(memory_space=pltpu.VMEM)
    dma = pltpu.SemaphoreType.DMA
    *outs, filt = pl.pallas_call(
        functools.partial(kernel, n, grps, width, chunks, size),
        out_shape=(wide, wide, wide, wide, jax.ShapeDtypeStruct((grps, chunks, h, gpc, size), F32)),
        in_specs=[vmem] * 5,
        out_specs=(vmem,) * 5,
        scratch_shapes=[
            pltpu.VMEM((rows_grp, size), BF),
            pltpu.VMEM((rows_grp, size), BF),
            pltpu.VMEM((chunks, n, cw, size), BF),
            pltpu.VMEM((chunks, n, cw, size), BF),
            pltpu.VMEM((n, groups, size), F32),
            pltpu.VMEM((chunks, h, cw, size), BF),
            pltpu.VMEM((chunks, h, cw, size), BF),
            pltpu.VMEM((rows_grp, size), BF),
            pltpu.VMEM((rows_grp, size), BF),
            pltpu.VMEM((chunks, n, gpc, size), F32),
            pltpu.VMEM((chunks, n, gpc, size), F32),
            pltpu.VMEM((chunks, h, gpc, size), F32),
            pltpu.VMEM((grps, chunks, h, gpc, size), F32),
            pltpu.VMEM((HALF, HALF + seq), BF),
            pltpu.VMEM((3 * rows, size), BF),
            pltpu.VMEM((rows, size), F32),
            pltpu.VMEM((rows, size), F32),
            dma, dma,
            dma((chunks,)), dma((chunks,)), dma((chunks,)), dma((chunks,)),
            dma((chunks,)), dma((chunks,)), dma((chunks,)), dma((chunks,)),
            dma((chunks,)), dma((chunks,)),
            dma, dma,
        ],
        compiler_params=pltpu.CompilerParams(
            collective_id=0, has_side_effects=True, vmem_limit_bytes=56 * 1024 * 1024
        ),
    )(query_in, key_in, value_in, cotangent, mine.reshape(h, groups, size))
    grad_filter = jnp.transpose(filt, (0, 2, 1, 3, 4)).reshape(grps * group_dev, size)
    return (*outs, grad_filter)


def solution(mesh):
    wide = P("grp", "ctx")
    return jax.shard_map(
        per_device,
        mesh=mesh,
        in_specs=(wide, wide, wide, wide, P(None, "ctx")),
        out_specs=(wide, wide, wide, wide, P(None, "ctx")),
        check_vma=False,
    )
```

```python
import functools
import math

import jax
import jax.numpy as jnp
from jax import lax
from jax.experimental import pallas as pl
from jax.experimental.pallas import tpu as pltpu
from jax.sharding import PartitionSpec as P

GROUP_CH = 16
HALF = 128
BF = jnp.bfloat16
F32 = jnp.float32
MESH = pl.DeviceIdType.MESH
CHUNKS = 4


def build_toeplitz(taps_row, toep):
    seq = taps_row.shape[1]
    wide = jnp.broadcast_to(taps_row, (HALF, seq))
    rolled = pltpu.roll(wide, 0, 1, stride=1, stride_axis=0)
    row = lax.broadcasted_iota(jnp.int32, (HALF, HALF), 0)
    lane = lax.broadcasted_iota(jnp.int32, (HALF, HALF), 1)
    toep[:, :HALF] = jnp.zeros((HALF, HALF), BF)
    toep[:, HALF : 2 * HALF] = jnp.where(lane >= row, rolled[:, :HALF], 0.0).astype(BF)
    toep[:, 2 * HALF :] = rolled[:, HALF:].astype(BF)


def toeplitz_block(toep, lag, size):
    at = lag * size
    return jnp.concatenate(
        [toep[:, HALF + at : HALF + at + size], toep[:, at : at + size]], axis=0
    )


def diagonal_sums(pieces, seq):
    total = None
    for r in range(HALF // 8):
        line = jnp.concatenate([p[8 * r : 8 * r + 8] for p in pieces], axis=1)
        if r:
            line = pltpu.roll(line, seq + HALF - 8 * r, 1)
        total = line if total is None else total + line
    out = total[0:1, :]
    for s in range(1, 8):
        out = out + pltpu.roll(total, seq + HALF - s, 1)[s : s + 1, :]
    return out[:, :seq]


def nn_dot(a, b):
    return jnp.dot(a, b, preferred_element_type=F32)


def nt_dot(a, b):
    return lax.dot_general(a, b, (((1,), (1,)), ((), ())), preferred_element_type=F32)


def kernel(
    n, grps, width, chunks, size,
    q_ref, k_ref, v_ref, c_ref, f_ref,
    conv_ref, dmix_ref, gf_ref,
    mixed_st, dconv_st, xb, db, tapb, conv_st, dmix_st, conv_rc, dmix_rc,
    part_st, part_rc, filt_st, filt_rc, toep, dpad, acc, acc2,
    tap_s, tap_r, x_s, x_r, d_s, d_r, cv_s, cv_r, dm_s, dm_r, pt_s, pt_r, fl_s, fl_r,
):
    me = lax.axis_index("ctx")
    grp = lax.axis_index("grp")
    h = n // 2
    side, lane = me // h, lax.rem(me, h)
    cw = width // chunks
    gpc = cw // GROUP_CH
    rows = h * GROUP_CH
    seq = n * size

    barrier = pltpu.get_barrier_semaphore()

    @pl.loop(1, n)
    def _(r):
        pl.semaphore_signal(barrier, inc=1, device_id={"ctx": lax.rem(me + r, n)}, device_id_type=MESH)

    @pl.loop(1, grps)
    def _(r):
        pl.semaphore_signal(barrier, inc=1, device_id={"grp": lax.rem(grp + r, grps)}, device_id_type=MESH)

    def send(src, dst, ssem, rsem, to):
        pltpu.make_async_remote_copy(
            src_ref=src, dst_ref=dst, send_sem=ssem, recv_sem=rsem,
            device_id={"ctx": to}, device_id_type=MESH,
        ).start()

    def drain(ref, sem):
        pltpu.make_async_copy(ref, ref, sem).wait()

    def product(c):
        @pl.loop(0, h)
        def _(i):
            at = pl.ds(pl.multiple_of(i * width + c * cw, GROUP_CH), cw)
            mixed_st[at, :] = (k_ref[at, :].astype(F32) * v_ref[at, :].astype(F32)).astype(BF)
            dconv_st[at, :] = (c_ref[at, :].astype(F32) * q_ref[at, :].astype(F32)).astype(BF)

    def ship(c):
        def block(st, to):
            return st.at[pl.ds(pl.multiple_of(lax.rem(to, h) * width + c * cw, GROUP_CH), cw)]

        @pl.loop(0, h)
        def _(r):
            near = lax.rem(lane + r, h)
            apart = lax.rem(lane + r + h // 2, h)
            over = (1 - side) * h + near

            @pl.when(side == 0)
            def _():
                send(block(mixed_st, over), xb.at[c, me], x_s.at[c], x_r.at[c], over)

            @pl.when(side == 1)
            def _():
                send(block(dconv_st, over), db.at[c, me], d_s.at[c], d_r.at[c], over)

            @pl.when(r != h // 2)
            def _():
                to = side * h + apart
                send(block(mixed_st, to), xb.at[c, me], x_s.at[c], x_r.at[c], to)

            @pl.when(r != 0)
            def _():
                to = side * h + near
                send(block(dconv_st, to), db.at[c, me], d_s.at[c], d_r.at[c], to)

        own = pl.ds(pl.multiple_of(lane * width + c * cw, GROUP_CH), cw)
        xb[c, me] = mixed_st[own, :]
        db[c, me] = dconv_st[own, :]

    product(0)
    pl.semaphore_wait(barrier, n - 1 + grps - 1)

    @pl.loop(1, n)
    def _(r):
        to = lax.rem(me + r, n)
        send(f_ref.at[grp, lax.rem(to, h)], tapb.at[me], tap_s, tap_r, to)

    tapb[me] = f_ref[grp, lane]
    ship(0)

    @pl.loop(1, chunks)
    def _(c):
        product(c)
        ship(c)

    drain(tapb.at[pl.ds(0, n - 1)], tap_r)

    def finish(c, few, few_sem, many, many_sem):
        drain(few.at[c, pl.ds(0, h - 1)], few_sem.at[c])
        drain(many.at[c, pl.ds(0, n - 1)], many_sem.at[c])

    def arrived(c):
        @pl.when(side == 0)
        def _():
            finish(c, xb, x_r, db, d_r)

        @pl.when(side == 1)
        def _():
            finish(c, db, d_r, xb, x_r)

    def departed(c):
        @pl.when(side == 0)
        def _():
            finish(c, db, d_s, xb, x_s)

        @pl.when(side == 1)
        def _():
            finish(c, xb, x_s, db, d_s)

    dpad[rows:] = jnp.zeros((2 * rows, size), BF)

    def group(c, g):
        at = pl.ds(pl.multiple_of(g * GROUP_CH, GROUP_CH), GROUP_CH)
        mine = pl.ds(side * h, h)
        x = xb[c, mine, at, :].reshape(rows, size)
        d = db[c, mine, at, :].reshape(rows, size)
        which = pl.ds(c * gpc + g, 1)
        build_toeplitz(jnp.concatenate([tapb[j, which, :] for j in range(n)], axis=1), toep)
        dpad[:rows] = d

        @pl.when(side == 0)
        def _():
            dpad[rows : 2 * rows] = db[c, h:, at, :].reshape(rows, size)

        xt = x.T
        pieces = []
        held = None
        for lag in range(n):
            prod = nn_dot(xt, dpad[lag * GROUP_CH : lag * GROUP_CH + rows])
            top, bottom = prod[:HALF], prod[HALF:]
            if held is not None:
                pieces.append(held + bottom[:, :HALF])
            pieces.append(top[:, :HALF] + bottom[:, HALF:])
            held = top[:, HALF:]
        pieces.append(held)
        pieces.append(jnp.zeros((HALF, HALF), F32))
        sums = diagonal_sums(pieces, seq)
        for j in range(n):
            part_st[c, j, pl.ds(g, 1), :] = sums[:, j * size : (j + 1) * size]
        for lag in range(h):
            keep = rows - lag * GROUP_CH
            block = toeplitz_block(toep, lag, size)
            fwd = nn_dot(x[:keep], block)
            bwd = nt_dot(d[rows - keep :], block)
            if lag == 0:
                acc[...] = fwd
                acc2[...] = bwd
            else:
                acc[rows - keep :] += fwd
                acc2[:keep] += bwd

        @pl.when(side == 1)
        def _():
            low = xb[c, :h, at, :].reshape(rows, size)
            for lag in range(1, n):
                block = toeplitz_block(toep, lag, size)
                cut = GROUP_CH * (lag if lag <= h else lag - h)
                if lag <= h:
                    acc[:cut] += nn_dot(low[rows - cut :], block)
                else:
                    acc[cut:] += nn_dot(low[: rows - cut], block)

        @pl.when(side == 0)
        def _():
            high = db[c, h:, at, :].reshape(rows, size)
            for lag in range(1, n):
                block = toeplitz_block(toep, lag, size)
                cut = GROUP_CH * (lag if lag <= h else lag - h)
                if lag <= h:
                    acc2[rows - cut :] += nt_dot(high[:cut], block)
                else:
                    acc2[: rows - cut] += nt_dot(high[cut:], block)

        conv_st[c, :, at, :] = acc[...].astype(BF).reshape(h, GROUP_CH, size)
        dmix_st[c, :, at, :] = acc2[...].astype(BF).reshape(h, GROUP_CH, size)

    @pl.loop(0, chunks)
    def _(c):
        arrived(c)

        @pl.loop(0, gpc)
        def _(g):
            group(c, g)

        own = pl.ds(pl.multiple_of(lane * width + c * cw, GROUP_CH), cw)

        @pl.loop(0, h)
        def _(r):
            near = lax.rem(lane + r, h)
            apart = lax.rem(lane + r + h // 2, h)

            @pl.when(r != h // 2)
            def _():
                send(conv_st.at[c, apart], conv_rc.at[own], cv_s.at[c], cv_r.at[c], side * h + apart)

            @pl.when(r != 0)
            def _():
                send(dmix_st.at[c, near], dmix_rc.at[own], dm_s.at[c], dm_r.at[c], side * h + near)

        @pl.loop(1, n)
        def _(r):
            to = lax.rem(me + r, n)
            send(part_st.at[c, to], part_rc.at[c, me], pt_s.at[c], pt_r.at[c], to)

        conv_rc[own, :] = conv_st[c, lane]
        dmix_rc[own, :] = dmix_st[c, lane]
        part_rc[c, me] = part_st[c, me]

    @pl.loop(0, chunks)
    def _(c):
        drain(conv_st.at[c, pl.ds(0, h - 1)], cv_r.at[c])
        drain(dmix_st.at[c, pl.ds(0, h - 1)], dm_r.at[c])

        @pl.loop(0, h)
        def _(i):
            at = pl.ds(pl.multiple_of(i * width + c * cw, GROUP_CH), cw)
            conv_ref[at, :] = conv_rc[at, :]
            dmix_ref[at, :] = dmix_rc[at, :]

    scale = 1.0 / math.sqrt(GROUP_CH * seq)

    @pl.loop(0, chunks)
    def _(c):
        drain(part_st.at[c, pl.ds(0, n - 1)], pt_r.at[c])
        filt_st[c] = (part_rc[c, :h] + part_rc[c, h:]) * scale

    @pl.loop(1, grps)
    def _(r):
        pltpu.make_async_remote_copy(
            src_ref=filt_st, dst_ref=filt_rc.at[grp], send_sem=fl_s, recv_sem=fl_r,
            device_id={"grp": lax.rem(grp + r, grps)}, device_id_type=MESH,
        ).start()

    filt_rc[grp] = filt_st[...]

    drain(tapb.at[pl.ds(0, n - 1)], tap_s)

    @pl.loop(0, chunks)
    def _(c):
        departed(c)
        drain(conv_st.at[c, pl.ds(0, h - 1)], cv_s.at[c])
        drain(dmix_st.at[c, pl.ds(0, h - 1)], dm_s.at[c])
        drain(part_st.at[c, pl.ds(0, n - 1)], pt_s.at[c])

    drain(filt_rc.at[pl.ds(0, grps - 1)], fl_r)
    gf_ref[...] = filt_rc[...]
    drain(filt_rc.at[pl.ds(0, grps - 1)], fl_s)


def steps_of(rows):
    return max(1, rows // 512)


def gate_step(q_ref, k_ref, v_ref, c_ref, conv_ref, dmix_ref, filt_ref,
              gated_ref, gq_ref, gk_ref, gv_ref, gf_ref):
    conv, dmixed = conv_ref[...].astype(F32), dmix_ref[...].astype(F32)
    gated_ref[...] = (q_ref[...].astype(F32) * conv).astype(BF)
    gq_ref[...] = (c_ref[...].astype(F32) * conv).astype(BF)
    gk_ref[...] = (dmixed * v_ref[...].astype(F32)).astype(BF)
    gv_ref[...] = (dmixed * k_ref[...].astype(F32)).astype(BF)

    @pl.when(pl.program_id(0) == 0)
    def _():
        grps, chunks, h, gpc, _ = filt_ref.shape
        for y in range(grps):
            for i in range(h):
                for c in range(chunks):
                    at = ((y * h + i) * chunks + c) * gpc
                    gf_ref[at : at + gpc] = filt_ref[y, c, i]


def per_device(query_in, key_in, value_in, cotangent, conv_filter):
    rows_grp, size = query_in.shape
    n, grps = lax.axis_size("ctx"), lax.axis_size("grp")
    h = n // 2
    seq = size * n
    width = rows_grp // h
    groups = width // GROUP_CH
    chunks = min(CHUNKS, groups)
    cw = width // chunks
    gpc = groups // chunks
    group_dev = rows_grp // GROUP_CH
    rows = h * GROUP_CH
    wide = jax.ShapeDtypeStruct((rows_grp, size), BF)
    vmem = pl.BlockSpec(memory_space=pltpu.VMEM)
    dma = pltpu.SemaphoreType.DMA
    conv, dmixed, filt = pl.pallas_call(
        functools.partial(kernel, n, grps, width, chunks, size),
        out_shape=(wide, wide, jax.ShapeDtypeStruct((grps, chunks, h, gpc, size), F32)),
        in_specs=[vmem] * 5,
        out_specs=(vmem,) * 3,
        scratch_shapes=[
            pltpu.VMEM((rows_grp, size), BF),
            pltpu.VMEM((rows_grp, size), BF),
            pltpu.VMEM((chunks, n, cw, size), BF),
            pltpu.VMEM((chunks, n, cw, size), BF),
            pltpu.VMEM((n, groups, size), F32),
            pltpu.VMEM((chunks, h, cw, size), BF),
            pltpu.VMEM((chunks, h, cw, size), BF),
            pltpu.VMEM((rows_grp, size), BF),
            pltpu.VMEM((rows_grp, size), BF),
            pltpu.VMEM((chunks, n, gpc, size), F32),
            pltpu.VMEM((chunks, n, gpc, size), F32),
            pltpu.VMEM((chunks, h, gpc, size), F32),
            pltpu.VMEM((grps, chunks, h, gpc, size), F32),
            pltpu.VMEM((HALF, HALF + seq), BF),
            pltpu.VMEM((3 * rows, size), BF),
            pltpu.VMEM((rows, size), F32),
            pltpu.VMEM((rows, size), F32),
            dma, dma,
            dma((chunks,)), dma((chunks,)), dma((chunks,)), dma((chunks,)),
            dma((chunks,)), dma((chunks,)), dma((chunks,)), dma((chunks,)),
            dma((chunks,)), dma((chunks,)),
            dma, dma,
        ],
        compiler_params=pltpu.CompilerParams(
            collective_id=0, has_side_effects=True, vmem_limit_bytes=56 * 1024 * 1024
        ),
    )(query_in, key_in, value_in, cotangent, conv_filter.reshape(grps, h, groups, size))
    tall = rows_grp // steps_of(rows_grp)
    part_spec = pl.BlockSpec((tall, size), lambda i: (i, 0))
    return pl.pallas_call(
        gate_step,
        grid=(steps_of(rows_grp),),
        out_shape=(wide, wide, wide, wide, jax.ShapeDtypeStruct((grps * group_dev, size), F32)),
        in_specs=[part_spec] * 6 + [pl.BlockSpec(filt.shape, lambda i: (0,) * 5)],
        out_specs=(part_spec,) * 4
        + (pl.BlockSpec((grps * group_dev, size), lambda i: (0, 0)),),
        compiler_params=pltpu.CompilerParams(vmem_limit_bytes=32 * 1024 * 1024),
    )(query_in, key_in, value_in, cotangent, conv, dmixed, filt)


def solution(mesh):
    wide = P("grp", "ctx")
    return jax.shard_map(
        per_device,
        mesh=mesh,
        in_specs=(wide, wide, wide, wide, P(None, "ctx")),
        out_specs=(wide, wide, wide, wide, P(None, "ctx")),
        check_vma=False,
    )
```
